256 devices in a mesh: dp: 256 (over x, y, z, core).
Axes of the slice: x: 4, y: 4, z: 8, core: 2. Of those that a mesh axis runs over, the one named last changes fastest.
Arguments:
- pooled: bfloat16 [32768, 1152], P('dp'), may hold values from -6 to 6
- captions: bfloat16 [32768, 1152], P('dp'), may hold values from -0.1796875 to 0.1796875
- norm_gain_vector: float32 [1152], replicated, may hold values from 0.5 to 1.5
- up_matrix: bfloat16 [1152, 2304], replicated, may hold values from -0.1875 to 0.1875
- up_bias_vector: float32 [2304], replicated, may hold values from -3 to 3
- down_matrix: bfloat16 [2304, 1152], replicated, may hold values from -0.125 to 0.125
- log_scale: float32 [1], replicated, may hold values from 1.5 to 2.5
- logit_bias: float32 [1], replicated, may hold values from -4 to -1
Outputs:
- caption_grad: float32 [32768, 1152], P('dp')
- pooled_gradient: float32 [32768, 1152], P('dp')
- gain_grad: float32 [1152], replicated
- up_bias_grad: float32 [2304], P('dp')
The draws below stay inside these ranges and needn't reach their ends.
All inputs are finite; a program needn't handle non-finite values.
Results may differ from the reference program's by a relative error of at most 0.007.
Values may be sent and summed in bfloat16 or wider, within the bound.
A program may use at most 64 MiB of HBM per device.

```python
import jax
import jax.numpy as jnp
from jax import lax

D = 1152
F = 2304
TOK_DEV = 128
SHIFTS = 4
BATCH = 32768
N_DP = 256


def steps_of(own_key, extent, pieces, low, top_value):
    factor_of, own = 1.0, jax.random.fold_in(own_key, 6)
    for dim, blocks in pieces:
        steps = jnp.exp(jax.random.uniform(jax.random.fold_in(own, dim), (blocks,), jnp.float32, low / len(pieces), top_value / len(pieces)))
        factor_of = factor_of * jnp.repeat(steps, extent[dim] // blocks).reshape([-1 if axis == dim else 1 for axis in range(len(extent))])
    return factor_of


def centred(rng, dims, width, limit, split=(), kind=jnp.bfloat16):
    drawn = jax.random.normal(rng, dims, jnp.float32) * width
    if len(split) > 0:
        drawn = steps_of(rng, dims, split, -0.22, 0.18) * drawn
    return jnp.clip(drawn, min=-limit, max=limit).astype(kind)


def setup_inputs(seed: int = 0) -> dict:
    keys = jax.random.split(jax.random.key(seed), 9)
    return {
        "pooled": centred(keys[0], (BATCH, D), 1.0, 6.0, ((0, 256),)),
        "captions": centred(keys[1], (BATCH, D), 0.03, 0.1796875, ((0, 256),)),
        "norm_gain_vector": jnp.clip(1.0 + 0.1 * jax.random.normal(keys[2], (D,), jnp.float32), 0.5, 1.5),
        "up_matrix": centred(keys[3], (D, F), D ** -0.5, 0.1875),
        "up_bias_vector": centred(keys[4], (F,), 0.5, 3.0, (), jnp.float32),
        "down_matrix": centred(keys[5], (F, D), F ** -0.5, 0.125),
        "log_scale": jnp.clip(jax.random.uniform(keys[6], (1,), jnp.float32, 1.5, 2.5), 1.5, 2.5),
        "logit_bias": jnp.clip(jax.random.uniform(keys[7], (1,), jnp.float32, -4.0, -1.0), -4.0, -1.0),
    }


epsilon = 1e-06

def image_mlp_block(image_feature_rows, norm_gain_vector, up_matrix, up_bias_vector, down_matrix):
    feats = image_feature_rows.astype(jnp.float32)
    average = lax.optimization_barrier(jnp.mean(feats, axis=1, keepdims=True))
    centered_rows = feats - average
    variance = lax.optimization_barrier(jnp.mean(centered_rows * centered_rows, axis=1, keepdims=True))
    inverse_deviation = lax.rsqrt(variance + epsilon)
    standardized_rows = centered_rows * inverse_deviation
    normed_rows = (standardized_rows * norm_gain_vector).astype(jnp.bfloat16)
    hidden_preactivation = jnp.dot(normed_rows, up_matrix, preferred_element_type=jnp.float32) + up_bias_vector
    hidden = jax.nn.gelu(hidden_preactivation).astype(jnp.bfloat16)
    embed = feats + jnp.dot(hidden, down_matrix, preferred_element_type=jnp.float32)
    image_row_norm = jnp.sqrt(lax.optimization_barrier(jnp.sum(embed * embed, axis=1, keepdims=True)) + epsilon)
    image_unit_rows = embed / image_row_norm
    return (standardized_rows, inverse_deviation, hidden_preactivation, image_row_norm, image_unit_rows)

def band_terms(image_unit_rows, candidates, logit_scale, offset_bias, row_count):
    image_half = image_unit_rows.astype(jnp.bfloat16)
    logits = logit_scale * lax.dot_general(image_half, candidates, (((1,), (1,)), ((), ())), preferred_element_type=jnp.float32) + offset_bias
    row_ids = lax.broadcasted_iota(jnp.int32, logits.shape, 0)
    col_ids = lax.broadcasted_iota(jnp.int32, logits.shape, 1)
    labels = jnp.where(col_ids == row_ids + SHIFTS * row_count, 1.0, -1.0).astype(jnp.float32)
    dlogit = (-labels * jax.nn.sigmoid(-labels * logits)).astype(jnp.bfloat16)
    image_gradient = logit_scale * jnp.dot(dlogit, candidates, preferred_element_type=jnp.float32)
    raw_terms = lax.dot_general(dlogit, image_half, (((0,), (0,)), ((), ())), preferred_element_type=jnp.float32)
    return (image_gradient, raw_terms)

def mlp_block_backward(image_gradient, image_unit_rows, image_row_norm, hidden_preactivation, standardized_rows, inverse_deviation, norm_gain_vector, up_matrix, down_matrix):
    along = lax.optimization_barrier(jnp.sum(image_unit_rows * image_gradient, axis=1, keepdims=True))
    embed_gradient = ((image_gradient - image_unit_rows * along) / image_row_norm).astype(jnp.bfloat16)
    dhidden = lax.dot_general(embed_gradient, down_matrix, (((1,), (1,)), ((), ())), preferred_element_type=jnp.float32)
    dpreact = jax.vjp(jax.nn.gelu, hidden_preactivation)[1](dhidden)[0].astype(jnp.bfloat16)
    bias_parts_list = lax.optimization_barrier(jnp.sum(dpreact.astype(jnp.float32), axis=0))
    normed_gradient = lax.dot_general(dpreact, up_matrix, (((1,), (1,)), ((), ())), preferred_element_type=jnp.float32)
    gain_parts_list = lax.optimization_barrier(jnp.sum(normed_gradient * standardized_rows, axis=0))
    standardized_gradient = normed_gradient * norm_gain_vector
    first_output = lax.optimization_barrier(jnp.mean(standardized_gradient, axis=1, keepdims=True))
    second_output = lax.optimization_barrier(jnp.mean(standardized_gradient * standardized_rows, axis=1, keepdims=True))
    pooled_feature_rows = embed_gradient.astype(jnp.float32) + inverse_deviation * (standardized_gradient - first_output - standardized_rows * second_output)
    return (pooled_feature_rows, gain_parts_list, bias_parts_list)

def reference(pooled, captions, norm_gain_vector, up_matrix, up_bias_vector, down_matrix, log_scale, logit_bias):
    logit_scale = jnp.exp(log_scale[0])
    offset_bias = logit_bias[0]
    text_f = captions.astype(jnp.float32)
    text_norm = jnp.sqrt(lax.optimization_barrier(jnp.sum(text_f * text_f, axis=1, keepdims=True)) + epsilon)
    text_unit = text_f / text_norm
    text_half = text_unit.astype(jnp.bfloat16)

    def per_device(carry, device):
        gain_total, bias_total, text_total, pooled_total = carry
        image_feature_rows = lax.dynamic_slice_in_dim(pooled, device * TOK_DEV, TOK_DEV, 0)
        standardized_rows, inverse_deviation, hidden_preactivation, image_row_norm, image_unit_rows = image_mlp_block(image_feature_rows, norm_gain_vector, up_matrix, up_bias_vector, down_matrix)
        starts = [(device + offset) % N_DP * TOK_DEV for offset in range(-SHIFTS, SHIFTS + 1)]
        candidates = jnp.concatenate([lax.dynamic_slice_in_dim(text_half, begin, TOK_DEV, 0) for begin in starts], axis=0)
        image_gradient, raw_terms = band_terms(image_unit_rows, candidates, logit_scale, offset_bias, TOK_DEV)
        for index, begin in enumerate(starts):
            current = lax.dynamic_slice_in_dim(text_total, begin, TOK_DEV, 0)
            text_total = lax.dynamic_update_slice_in_dim(text_total, current + raw_terms[index * TOK_DEV:(index + 1) * TOK_DEV], begin, 0)
        pooled_feature_rows, gain_parts_list, bias_parts_list = mlp_block_backward(image_gradient, image_unit_rows, image_row_norm, hidden_preactivation, standardized_rows, inverse_deviation, norm_gain_vector, up_matrix, down_matrix)
        pooled_total = lax.dynamic_update_slice_in_dim(pooled_total, pooled_feature_rows, device * TOK_DEV, 0)
        return ((gain_total + gain_parts_list, bias_total + bias_parts_list, text_total, pooled_total), None)
    start_carry = (jnp.zeros((D,), jnp.float32), jnp.zeros((F,), jnp.float32), jnp.zeros((BATCH, D), jnp.float32), jnp.zeros((BATCH, D), jnp.float32))
    (gain_grad, up_bias_grad, text_total, pooled_gradient), _ = lax.scan(per_device, start_carry, jnp.arange(N_DP, dtype=jnp.int32))
    dtext = logit_scale * text_total
    caption_grad = (dtext - text_unit * lax.optimization_barrier(jnp.sum(text_unit * dtext, axis=1, keepdims=True))) / text_norm
    return (caption_grad, pooled_gradient, gain_grad, up_bias_grad)
```

```python
import functools

import jax
import jax.numpy as jnp
from jax import lax
from jax.experimental import pallas as pl
from jax.experimental.pallas import tpu as pltpu
from jax.sharding import PartitionSpec as P

MESH = pl.DeviceIdType.MESH
EPS = 1e-06
CHUNKS = 2
TILE = 256
NT = (((1,), (1,)), ((), ()))
BEHIND, AHEAD, FAR_BEHIND, FAR_AHEAD, SIBLING, SIB_BEHIND, SIB_AHEAD, SIB_FAR = range(8)


def dot(a, b, dims=(((1,), (0,)), ((), ()))):
    return lax.dot_general(a, b, dims, preferred_element_type=jnp.float32)


def kernel(
    n,
    nz,
    pooled_hbm,
    captions_hbm,
    gain_hbm,
    up_hbm,
    bias_hbm,
    down_hbm,
    log_scale_ref,
    logit_bias_ref,
    caption_out,
    pooled_out,
    gain_out,
    bias_out,
    pooled,
    captions,
    gain,
    up,
    bias,
    down,
    blocks,
    xhat,
    normed,
    slope,
    unit,
    dembed,
    acc,
    dtext,
    halves,
    from_sibling,
    plane,
    line,
    whole,
    load_sem,
    send_sem,
    recv_sem,
    pair_send,
    pair_recv,
    plane_send,
    plane_recv,
    line_send,
    line_recv,
):
    rows, width = pooled.shape
    hidden_width = up.shape[1]
    nxy = n // (2 * nz)
    part = rows // CHUNKS
    half_width = halves.shape[2]
    share = hidden_width // n
    me = lax.axis_index("dp")
    core = lax.rem(me, 2)
    z = lax.rem(me // 2, nz)
    xy = me // (2 * nz)
    sibling = me + 1 - 2 * core
    ahead, behind = lax.rem(me + 2, n), lax.rem(me + n - 2, n)
    plane_peers = [lax.rem(me + 2 * nz * k, n) for k in range(1, nxy)]
    line_peers = [xy * 2 * nz + lax.rem(z + k, nz) * 2 + core for k in range(1, nz)]

    barrier = pltpu.get_barrier_semaphore()
    greeted = [ahead, behind, sibling] + plane_peers + line_peers
    for peer in greeted:
        pl.semaphore_signal(barrier, inc=1, device_id=(peer,), device_id_type=MESH)

    weight_parts = 3
    wide = hidden_width // weight_parts
    loads = [
        pltpu.make_async_copy(captions_hbm, captions, load_sem.at[0]),
        pltpu.make_async_copy(pooled_hbm, pooled, load_sem.at[1]),
        pltpu.make_async_copy(gain_hbm, gain, load_sem.at[2]),
        pltpu.make_async_copy(bias_hbm, bias, load_sem.at[3]),
    ]
    up_loads, down_loads = [], []
    for p in range(weight_parts):
        span = pl.ds(p * wide, wide)
        up_loads.append(
            pltpu.make_async_copy(up_hbm.at[:, span], up.at[:, span], load_sem.at[4 + 2 * p])
        )
        down_loads.append(
            pltpu.make_async_copy(down_hbm.at[span], down.at[span], load_sem.at[5 + 2 * p])
        )
        loads += [up_loads[-1], down_loads[-1]]
    for load in loads:
        load.start()

    def move(kind, side, source, target, device, c):
        span = pl.ds(c * part, part)
        return pltpu.make_async_remote_copy(
            src_ref=blocks.at[side, source, span],
            dst_ref=blocks.at[side, target, span],
            send_sem=send_sem.at[side, kind, c],
            recv_sem=recv_sem.at[side, kind, c],
            device_id=(device,),
            device_id_type=MESH,
        )

    def route(kind, side, c):
        if kind == BEHIND:
            return move(kind, side, 4 + core, 2 + core, ahead, c)
        if kind == AHEAD:
            return move(kind, side, 4 + core, 6 + core, behind, c)
        if kind == FAR_BEHIND:
            return move(kind, side, 2 + core, core, ahead, c)
        if kind == FAR_AHEAD:
            return move(kind, side, 6 + core, 8 + core, behind, c)
        if kind == SIBLING:
            return move(kind, side, 4 + core, 4 + core, sibling, c)
        if kind == SIB_BEHIND:
            return move(kind, side, 2 + core, 2 + core, sibling, c)
        if kind == SIB_AHEAD:
            return move(kind, side, 6 + core, 6 + core, sibling, c)
        return move(kind, side, 8 - 7 * core, 8 - 7 * core, sibling, c)

    def start(kinds, side, c):
        for kind in kinds:
            route(kind, side, c).start()

    def arrived(kinds, side, c):
        for kind in kinds:
            route(kind, side, c).wait_recv()

    TEXT, IMAGE = 0, 1
    log_scale = jnp.full((rows, rows), log_scale_ref[0], jnp.float32)
    scale = jnp.exp(log_scale)
    scale_column = scale[:, :1]
    offset = logit_bias_ref[0]

    loads[0].wait()
    text = captions[...].astype(jnp.float32)
    text_norm = jnp.sqrt(jnp.sum(text * text, axis=1, keepdims=True) + EPS)
    blocks[TEXT, 4 + core] = (text / text_norm).astype(jnp.bfloat16)
    pl.semaphore_wait(barrier, len(greeted))
    for c in range(CHUNKS):
        start([BEHIND, AHEAD, SIBLING], TEXT, c)

    loads[1].wait()
    loads[2].wait()
    loads[3].wait()
    feats = pooled[...].astype(jnp.float32)
    centered = feats - jnp.mean(feats, axis=1, keepdims=True)
    variance = jnp.mean(centered * centered, axis=1, keepdims=True)
    rstd = lax.rsqrt(variance + EPS)
    xhat[...] = centered * rstd
    normed[...] = (xhat[...] * gain[...]).astype(jnp.bfloat16)
    acc[...] = feats

    def forward(j, carry):
        span = pl.ds(pl.multiple_of(j * TILE, TILE), TILE)
        x = dot(normed[...], up[:, span]) + bias[:, span]
        c0, c1 = 0.7978845608028654, 0.044715
        square = x * x
        t = jnp.tanh(c0 * x * (1.0 + c1 * square))
        slope[:, span] = 0.5 * (1.0 + t) + (0.5 * c0) * x * (1.0 - t * t) * (
            1.0 + (3.0 * c1) * square
        )
        hidden = (0.5 * x * (1.0 + t)).astype(jnp.bfloat16)
        acc[...] += dot(hidden, down[span])
        return carry

    tiles = wide // TILE
    for p in range(weight_parts):
        up_loads[p].wait()
        down_loads[p].wait()
        lax.fori_loop(p * tiles, (p + 1) * tiles, forward, 0)
        if p == 1:
            arrived([BEHIND, AHEAD], TEXT, 0)
            start([FAR_BEHIND, FAR_AHEAD, SIB_BEHIND, SIB_AHEAD], TEXT, 0)
    embed = acc[...]
    image_norm = jnp.sqrt(jnp.sum(embed * embed, axis=1, keepdims=True) + EPS)
    unit[...] = embed / image_norm
    blocks[IMAGE, 4 + core] = unit[...].astype(jnp.bfloat16)
    for c in range(1, CHUNKS):
        arrived([BEHIND, AHEAD], TEXT, c)
        start([FAR_BEHIND, FAR_AHEAD, SIB_BEHIND, SIB_AHEAD], TEXT, c)
    for c in range(CHUNKS):
        start([BEHIND, AHEAD, SIBLING], IMAGE, c)

    def pair(total, side, slot, diagonal=False):
        other = blocks[side, slot]
        logits = scale * dot(blocks[1 - side, 4 + core], other, NT) + offset
        grad = jax.nn.sigmoid(logits)
        if diagonal:
            same = lax.broadcasted_iota(jnp.int32, logits.shape, 0) == lax.broadcasted_iota(
                jnp.int32, logits.shape, 1
            )
            grad = jnp.where(same, -jax.nn.sigmoid(-logits), grad)
        total[...] += dot(grad.astype(jnp.bfloat16), other)

    def settle(kinds, side):
        for c in range(CHUNKS):
            arrived(kinds, side, c)

    acc[...] = jnp.zeros_like(acc)
    pair(acc, TEXT, 4 + core, True)
    pair(acc, TEXT, 2 + core)
    pair(acc, TEXT, 6 + core)
    settle([SIBLING], TEXT)
    pair(acc, TEXT, 5 - core)
    settle([SIB_BEHIND, SIB_AHEAD], TEXT)
    pair(acc, TEXT, 3 - core)
    pair(acc, TEXT, 7 - core)
    for c in range(CHUNKS):
        arrived([FAR_BEHIND, FAR_AHEAD], TEXT, c)
        start([SIB_FAR], TEXT, c)
    pair(acc, TEXT, core)
    pair(acc, TEXT, 8 + core)
    settle([SIB_FAR], TEXT)
    pair(acc, TEXT, 1 + 7 * core)

    dimage = scale_column * acc[...]
    along = jnp.sum(unit[...] * dimage, axis=1, keepdims=True)
    dembed[...] = ((dimage - unit[...] * along) / image_norm).astype(jnp.bfloat16)
    acc[...] = jnp.zeros_like(acc)
    bias_parts = bias

    def backward(j, carry):
        span = pl.ds(pl.multiple_of(j * TILE, TILE), TILE)
        dpre = (dot(dembed[...], down[span], NT) * slope[:, span]).astype(jnp.bfloat16)
        bias_parts[:, span] = jnp.sum(dpre.astype(jnp.float32), axis=0, keepdims=True)
        acc[...] += dot(dpre, up[:, span], NT)
        return carry

    for p in range(weight_parts):
        lax.fori_loop(p * tiles, (p + 1) * tiles, backward, 0)
        if p == 1:
            arrived([BEHIND, AHEAD], IMAGE, 0)
            start([FAR_BEHIND, FAR_AHEAD, SIB_BEHIND, SIB_AHEAD], IMAGE, 0)

    gain_parts = jnp.sum(acc[...] * xhat[...], axis=0, keepdims=True)
    first = half_width - width
    second = hidden_width - first
    halves[0, :, :width] = gain_parts
    halves[0, :, width:] = bias_parts[:, :first]
    halves[1, :, :second] = bias_parts[:, first:]
    if second < half_width:
        halves[1, :, second:] = jnp.zeros((1, half_width - second), jnp.float32)

    def to_sibling(stage, source, target):
        return pltpu.make_async_remote_copy(
            src_ref=source,
            dst_ref=target,
            send_sem=pair_send.at[stage],
            recv_sem=pair_recv.at[stage],
            device_id=(sibling,),
            device_id_type=MESH,
        )

    give = to_sibling(0, halves.at[1 - core], from_sibling)
    give.start()

    for c in range(1, CHUNKS):
        arrived([BEHIND, AHEAD], IMAGE, c)
        start([FAR_BEHIND, FAR_AHEAD, SIB_BEHIND, SIB_AHEAD], IMAGE, c)
    dtext[...] = jnp.zeros_like(dtext)
    pair(dtext, IMAGE, 4 + core, True)

    give.wait_recv()
    plane[xy] = halves[core] + from_sibling[...]

    def in_plane(k):
        return pltpu.make_async_remote_copy(
            src_ref=plane.at[xy],
            dst_ref=plane.at[xy],
            send_sem=plane_send.at[k],
            recv_sem=plane_recv.at[k],
            device_id=(plane_peers[k],),
            device_id_type=MESH,
        )

    for k in range(nxy - 1):
        in_plane(k).start()

    dxhat = acc[...] * gain[...]
    mean1 = jnp.mean(dxhat, axis=1, keepdims=True)
    mean2 = jnp.mean(dxhat * xhat[...], axis=1, keepdims=True)
    pooled_out[...] = dembed[...].astype(jnp.float32) + rstd * (
        dxhat - mean1 - xhat[...] * mean2
    )
    pair(dtext, IMAGE, 2 + core)
    pair(dtext, IMAGE, 6 + core)

    for k in range(nxy - 1):
        in_plane(k).wait_recv()
    summed = plane[0]
    for k in range(1, nxy):
        summed = summed + plane[k]
    line[z] = summed

    def in_line(k):
        return pltpu.make_async_remote_copy(
            src_ref=line.at[z],
            dst_ref=line.at[z],
            send_sem=line_send.at[k],
            recv_sem=line_recv.at[k],
            device_id=(line_peers[k],),
            device_id_type=MESH,
        )

    for k in range(nz - 1):
        in_line(k).start()

    settle([SIBLING], IMAGE)
    pair(dtext, IMAGE, 5 - core)
    settle([SIB_BEHIND, SIB_AHEAD], IMAGE)
    pair(dtext, IMAGE, 3 - core)
    pair(dtext, IMAGE, 7 - core)

    for k in range(nz - 1):
        in_line(k).wait_recv()
    summed = line[0]
    for k in range(1, nz):
        summed = summed + line[k]
    whole[core] = summed
    share_out = to_sibling(1, whole.at[core], whole.at[core])
    share_out.start()

    for c in range(CHUNKS):
        arrived([FAR_BEHIND, FAR_AHEAD], IMAGE, c)
        start([SIB_FAR], IMAGE, c)
    pair(dtext, IMAGE, core)
    pair(dtext, IMAGE, 8 + core)
    share_out.wait_recv()
    gain_out[...] = whole[0, :, :width]
    bias_out[:, :first] = whole[0, :, width:]
    bias_out[:, first:] = whole[1, :, :second]
    settle([SIB_FAR], IMAGE)
    pair(dtext, IMAGE, 1 + 7 * core)

    text = captions[...].astype(jnp.float32)
    text_norm = jnp.sqrt(jnp.sum(text * text, axis=1, keepdims=True) + EPS)
    text_unit = text / text_norm
    dcaption = scale_column * dtext[...]
    caption_out[...] = (
        dcaption - text_unit * jnp.sum(text_unit * dcaption, axis=1, keepdims=True)
    ) / text_norm

    for side in (TEXT, IMAGE):
        for kind in range(8):
            for c in range(CHUNKS):
                route(kind, side, c).wait_send()
    give.wait_send()
    share_out.wait_send()
    for k in range(nxy - 1):
        in_plane(k).wait_send()
    for k in range(nz - 1):
        in_line(k).wait_send()


def local(
    n,
    nz,
    pooled,
    captions,
    norm_gain_vector,
    up_matrix,
    up_bias_vector,
    down_matrix,
    log_scale,
    logit_bias,
):
    rows, width = pooled.shape
    hidden_width = up_matrix.shape[1]
    nxy = n // (2 * nz)
    half_width = -(-(width + hidden_width) // 256) * 128
    f32, bf16 = jnp.float32, jnp.bfloat16
    vmem = pl.BlockSpec(memory_space=pltpu.VMEM)
    smem = pl.BlockSpec(memory_space=pltpu.SMEM)
    away = pl.BlockSpec(memory_space=pl.ANY)
    dma = pltpu.SemaphoreType.DMA
    caption_grad, pooled_gradient, gain_grad, bias_whole = pl.pallas_call(
        functools.partial(kernel, n, nz),
        out_shape=(
            jax.ShapeDtypeStruct((rows, width), f32),
            jax.ShapeDtypeStruct((rows, width), f32),
            jax.ShapeDtypeStruct((1, width), f32),
            jax.ShapeDtypeStruct((1, hidden_width), f32),
        ),
        in_specs=[away] * 6 + [smem] * 2,
        out_specs=(vmem,) * 4,
        scratch_shapes=[
            pltpu.VMEM((rows, width), bf16),
            pltpu.VMEM((rows, width), bf16),
            pltpu.VMEM((1, width), f32),
            pltpu.VMEM((width, hidden_width), bf16),
            pltpu.VMEM((1, hidden_width), f32),
            pltpu.VMEM((hidden_width, width), bf16),
            pltpu.VMEM((2, 10, rows, width), bf16),
            pltpu.VMEM((rows, width), f32),
            pltpu.VMEM((rows, width), bf16),
            pltpu.VMEM((rows, hidden_width), f32),
            pltpu.VMEM((rows, width), f32),
            pltpu.VMEM((rows, width), bf16),
            pltpu.VMEM((rows, width), f32),
            pltpu.VMEM((rows, width), f32),
            pltpu.VMEM((2, 1, half_width), f32),
            pltpu.VMEM((1, half_width), f32),
            pltpu.VMEM((nxy, 1, half_width), f32),
            pltpu.VMEM((nz, 1, half_width), f32),
            pltpu.VMEM((2, 1, half_width), f32),
            dma((10,)),
            dma((2, 8, CHUNKS)),
            dma((2, 8, CHUNKS)),
            dma((2,)),
            dma((2,)),
            dma((nxy - 1,)),
            dma((nxy - 1,)),
            dma((nz - 1,)),
            dma((nz - 1,)),
        ],
        compiler_params=pltpu.CompilerParams(
            collective_id=0, has_side_effects=True, vmem_limit_bytes=48 * 2**20
        ),
    )(
        pooled,
        captions,
        norm_gain_vector.reshape(1, width),
        up_matrix,
        up_bias_vector.reshape(1, hidden_width),
        down_matrix,
        log_scale,
        logit_bias,
    )
    share = hidden_width // n
    bias_rows = lax.dynamic_slice_in_dim(
        bias_whole.reshape(hidden_width), lax.axis_index("dp") * share, share, 0
    )
    return caption_grad, pooled_gradient, gain_grad.reshape(width), bias_rows


def solution(mesh, nz=8):
    placed = (P("dp", None), P("dp", None), P(), P(), P(), P(), P(), P())
    return jax.shard_map(
        functools.partial(local, mesh.shape["dp"], nz),
        mesh=mesh,
        in_specs=placed,
        out_specs=(P("dp", None), P("dp", None), P(), P("dp")),
        check_vma=False,
    )
```

```python
import functools

import jax
import jax.numpy as jnp
from jax import lax
from jax.experimental import pallas as pl
from jax.experimental.pallas import tpu as pltpu
from jax.sharding import PartitionSpec as P

MESH = pl.DeviceIdType.MESH
EPS = 1e-06
CHUNKS = 4
PARTS = 3
NT = (((1,), (1,)), ((), ()))
BEHIND, AHEAD, FAR_BEHIND, FAR_AHEAD, SIBLING, SIB_BEHIND, SIB_AHEAD, SIB_FAR = range(8)


def dot(a, b, dims=(((1,), (0,)), ((), ()))):
    return lax.dot_general(a, b, dims, preferred_element_type=jnp.float32)


def kernel(
    n,
    nz,
    pooled_hbm,
    captions_hbm,
    gain_hbm,
    up_hbm,
    bias_hbm,
    down_hbm,
    scalars,
    caption_out,
    pooled_out,
    gain_out,
    bias_out,
    pooled,
    captions,
    gain,
    up,
    bias,
    down,
    blocks,
    xhat,
    normed,
    slope,
    unit,
    text_unit,
    dembed,
    acc,
    dtext,
    partial,
    plane,
    line,
    caption_sem,
    load_sem,
    send_sem,
    recv_sem,
    plane_send,
    plane_recv,
    line_send,
    line_recv,
):
    rows, width = pooled.shape
    hidden_width = up.shape[1]
    nxy = n // (2 * nz)
    part = rows // CHUNKS
    group = 2 * nz
    slice_width = hidden_width // nxy
    me = lax.axis_index("dp")
    core = lax.rem(me, 2)
    xy = me // (2 * nz)
    sibling = me + 1 - 2 * core
    ahead, behind = lax.rem(me + 2, n), lax.rem(me + n - 2, n)
    plane_peers = [lax.rem(me + 2 * nz * k, n) for k in range(1, nxy)]
    place = lax.rem(me, group)
    line_peers = [xy * group + lax.rem(place + k, group) for k in range(1, group)]

    barrier = pltpu.get_barrier_semaphore()
    greeted = [ahead, behind] + plane_peers + line_peers
    for peer in greeted:
        pl.semaphore_signal(barrier, inc=1, device_id=(peer,), device_id_type=MESH)

    wide = hidden_width // PARTS
    loads = [
        pltpu.make_async_copy(pooled_hbm, pooled, load_sem.at[0]),
        pltpu.make_async_copy(gain_hbm, gain.at[0], load_sem.at[1]),
        pltpu.make_async_copy(bias_hbm, bias.at[0], load_sem.at[2]),
    ]
    up_loads, down_loads = [], []
    for p in range(PARTS):
        span = pl.ds(p * wide, wide)
        up_loads.append(
            pltpu.make_async_copy(up_hbm.at[:, span], up.at[:, span], load_sem.at[3 + 2 * p])
        )
        down_loads.append(
            pltpu.make_async_copy(down_hbm.at[span], down.at[span], load_sem.at[4 + 2 * p])
        )
        loads += [up_loads[-1], down_loads[-1]]
    caption_loads = []
    for c in range(CHUNKS):
        span = pl.ds(c * part, part)
        caption_loads.append(
            pltpu.make_async_copy(captions_hbm.at[span], captions.at[span], caption_sem.at[c])
        )
    for load in caption_loads + loads:
        load.start()

    def move(kind, side, source, target, device, c):
        span = pl.ds(c * part, part)
        return pltpu.make_async_remote_copy(
            src_ref=blocks.at[side, source, span],
            dst_ref=blocks.at[side, target, span],
            send_sem=send_sem.at[side, kind, c],
            recv_sem=recv_sem.at[side, kind, c],
            device_id=(device,),
            device_id_type=MESH,
        )

    def route(kind, side, c):
        if kind == BEHIND:
            return move(kind, side, 4 + core, 2 + core, ahead, c)
        if kind == AHEAD:
            return move(kind, side, 4 + core, 6 + core, behind, c)
        if kind == FAR_BEHIND:
            return move(kind, side, 2 + core, core, ahead, c)
        if kind == FAR_AHEAD:
            return move(kind, side, 6 + core, 8 + core, behind, c)
        if kind == SIBLING:
            return move(kind, side, 4 + core, 4 + core, sibling, c)
        if kind == SIB_BEHIND:
            return move(kind, side, 2 + core, 2 + core, sibling, c)
        if kind == SIB_AHEAD:
            return move(kind, side, 6 + core, 6 + core, sibling, c)
        return move(kind, side, 8 - 7 * core, 8 - 7 * core, sibling, c)

    def start(kinds, side, c):
        for kind in kinds:
            route(kind, side, c).start()

    def arrived(kinds, side, c):
        for kind in kinds:
            route(kind, side, c).wait_recv()

    TEXT, IMAGE = 0, 1
    first, second = range(CHUNKS // 2), range(CHUNKS // 2, CHUNKS)
    text_norms = []
    for c in range(CHUNKS):
        caption_loads[c].wait()
        span = pl.ds(c * part, part)
        text = captions[span].astype(jnp.float32)
        text_norms.append(jnp.sqrt(jnp.sum(text * text, axis=1, keepdims=True) + EPS))
        text_unit[span] = text / text_norms[c]
        blocks[TEXT, 4 + core, span] = text_unit[span].astype(jnp.bfloat16)
        if c == 0:
            pl.semaphore_wait(barrier, len(greeted))
        start([BEHIND, AHEAD] if c in first else [], TEXT, c)
    text_norm = jnp.concatenate(text_norms, axis=0)

    for load in loads[:3]:
        load.wait()
    scale = jnp.exp(jnp.broadcast_to(scalars[0:1, 0:1], (rows, 2 * rows)))
    scale_column = scale[:, :1]
    offset = scalars[1:2, 0:1]
    feats = pooled[...].astype(jnp.float32)
    centered = feats - jnp.mean(feats, axis=1, keepdims=True)
    variance = jnp.mean(centered * centered, axis=1, keepdims=True)
    rstd = lax.rsqrt(variance + EPS)
    xhat[...] = centered * rstd
    normed[...] = (xhat[...] * gain[...]).astype(jnp.bfloat16)
    acc[...] = feats
    for p in range(PARTS):
        span = pl.ds(p * wide, wide)
        up_loads[p].wait()
        x = dot(normed[...], up[:, span]) + bias[:, span]
        c0, c1 = 0.7978845608028654, 0.044715
        square = x * x
        t = jnp.tanh(c0 * x * (1.0 + c1 * square))
        slope[:, span] = 0.5 * (1.0 + t) + (0.5 * c0) * x * (1.0 - t * t) * (
            1.0 + (3.0 * c1) * square
        )
        hidden = (0.5 * x * (1.0 + t)).astype(jnp.bfloat16)
        down_loads[p].wait()
        acc[...] += dot(hidden, down[span])
        if p == 0:
            for c in second:
                start([BEHIND, AHEAD], TEXT, c)
            for c in range(CHUNKS):
                start([SIBLING], TEXT, c)
    embed = acc[...]
    image_norm = jnp.sqrt(jnp.sum(embed * embed, axis=1, keepdims=True) + EPS)
    unit[...] = embed / image_norm
    blocks[IMAGE, 4 + core] = unit[...].astype(jnp.bfloat16)

    def terms(total, side, other, own_chip=False):
        logits = scale[:, : other.shape[0]] * dot(blocks[1 - side, 4 + core], other, NT) + offset
        grad = jax.nn.sigmoid(logits)
        if own_chip:
            same = (
                lax.broadcasted_iota(jnp.int32, logits.shape, 1)
                == lax.broadcasted_iota(jnp.int32, logits.shape, 0) + core * rows
            )
            grad = jnp.where(same, -jax.nn.sigmoid(-logits), grad)
        total[...] += dot(grad.astype(jnp.bfloat16), other)

    def chip(total, side, place, own_chip=False):
        terms(total, side, blocks[side, pl.ds(2 * place, 2)].reshape(2 * rows, width), own_chip)

    def far_line(total, side):
        ends = [blocks[side, core], blocks[side, 8 + core]]
        terms(total, side, jnp.concatenate(ends, axis=0))

    def far_sibling(total, side):
        terms(total, side, blocks[side, 1 + 7 * core])

    def settle(kinds, side):
        for c in range(CHUNKS):
            arrived(kinds, side, c)

    def pass_on(side, chunks):
        for c in chunks:
            arrived([BEHIND, AHEAD], side, c)
            start([FAR_BEHIND, FAR_AHEAD, SIB_BEHIND, SIB_AHEAD], side, c)

    acc[...] = jnp.zeros_like(acc)
    pass_on(TEXT, first)
    for c in range(CHUNKS):
        start([SIBLING], IMAGE, c)
    settle([SIBLING], TEXT)
    chip(acc, TEXT, 2, True)
    pass_on(TEXT, second)
    settle([SIB_BEHIND, SIB_AHEAD], TEXT)
    chip(acc, TEXT, 1)
    chip(acc, TEXT, 3)
    for c in range(CHUNKS):
        for kind in (FAR_BEHIND, FAR_AHEAD):
            route(kind, TEXT, c).wait_send()
    for c in first:
        start([BEHIND, AHEAD], IMAGE, c)
    for c in range(CHUNKS):
        arrived([FAR_BEHIND, FAR_AHEAD], TEXT, c)
        start([SIB_FAR], TEXT, c)
    far_line(acc, TEXT)
    settle([SIB_FAR], TEXT)
    far_sibling(acc, TEXT)
    for c in second:
        start([BEHIND, AHEAD], IMAGE, c)

    dimage = scale_column * acc[...]
    along = jnp.sum(unit[...] * dimage, axis=1, keepdims=True)
    dembed[...] = ((dimage - unit[...] * along) / image_norm).astype(jnp.bfloat16)
    acc[...] = jnp.zeros_like(acc)
    bias_parts = bias
    for p in range(PARTS):
        span = pl.ds(p * wide, wide)
        dpre = (dot(dembed[...], down[span], NT) * slope[:, span]).astype(jnp.bfloat16)
        bias_parts[:, span] = jnp.sum(dpre.astype(jnp.float32), axis=0, keepdims=True)
        acc[...] += dot(dpre, up[:, span], NT)
        if p == 1:
            pass_on(IMAGE, first)

    partial[:, :, :width] = jnp.broadcast_to(
        jnp.sum(acc[...] * xhat[...], axis=0, keepdims=True)[None], (nxy, 1, width)
    )
    for q in range(nxy):
        partial[q, :, width : width + slice_width] = bias_parts[
            :, q * slice_width : (q + 1) * slice_width
        ]

    def in_plane(k):
        return pltpu.make_async_remote_copy(
            src_ref=partial.at[lax.rem(xy + k + 1, nxy)],
            dst_ref=plane.at[xy],
            send_sem=plane_send.at[k],
            recv_sem=plane_recv.at[k],
            device_id=(plane_peers[k],),
            device_id_type=MESH,
        )

    def in_line(k):
        return pltpu.make_async_remote_copy(
            src_ref=line.at[place],
            dst_ref=line.at[place],
            send_sem=line_send.at[k],
            recv_sem=line_recv.at[k],
            device_id=(line_peers[k],),
            device_id_type=MESH,
        )

    for k in range(nxy - 1):
        in_plane(k).start()
    plane[xy] = partial[xy]

    dxhat = acc[...] * gain[...]
    mean1 = jnp.mean(dxhat, axis=1, keepdims=True)
    mean2 = jnp.mean(dxhat * xhat[...], axis=1, keepdims=True)
    pooled_out[...] = dembed[...].astype(jnp.float32) + rstd * (
        dxhat - mean1 - xhat[...] * mean2
    )
    dtext[...] = jnp.zeros_like(dtext)
    settle([SIBLING], IMAGE)
    chip(dtext, IMAGE, 2, True)
    pass_on(IMAGE, second)
    settle([SIB_BEHIND, SIB_AHEAD], IMAGE)
    chip(dtext, IMAGE, 1)
    chip(dtext, IMAGE, 3)

    for k in range(nxy - 1):
        in_plane(k).wait_recv()
    line[place] = jnp.sum(plane[...], axis=0)
    for k in range(group - 1):
        in_line(k).start()

    for c in range(CHUNKS):
        arrived([FAR_BEHIND, FAR_AHEAD], IMAGE, c)
        start([SIB_FAR], IMAGE, c)
    far_line(dtext, IMAGE)
    settle([SIB_FAR], IMAGE)
    far_sibling(dtext, IMAGE)

    dcaption = scale_column * dtext[...]
    along = jnp.sum(text_unit[...] * dcaption, axis=1, keepdims=True)
    caption_out[...] = (dcaption - text_unit[...] * along) / text_norm

    for k in range(group - 1):
        in_line(k).wait_recv()
    summed = jnp.sum(line[...], axis=0)
    gain_out[...] = summed[:, :width]
    bias_out[...] = summed[:, width:]

    for side in (TEXT, IMAGE):
        for kind in range(8):
            for c in range(CHUNKS):
                if side == IMAGE or kind not in (FAR_BEHIND, FAR_AHEAD):
                    route(kind, side, c).wait_send()
    for k in range(nxy - 1):
        in_plane(k).wait_send()
    for k in range(group - 1):
        in_line(k).wait_send()


def finish(group, caption, pooled, gain, bias, caption_out, pooled_out, gain_out, bias_out, sems):
    share = bias_out.shape[0]
    part = caption.shape[0] // CHUNKS
    copies = [pltpu.make_async_copy(gain.at[0], gain_out, sems.at[2 * CHUNKS])]
    for c in range(CHUNKS):
        span = pl.ds(c * part, part)
        copies += [
            pltpu.make_async_copy(caption.at[span], caption_out.at[span], sems.at[2 * c]),
            pltpu.make_async_copy(pooled.at[span], pooled_out.at[span], sems.at[2 * c + 1]),
        ]
    for copy in copies:
        copy.start()
    total = bias.shape[1]
    begin = lax.rem(lax.axis_index("dp"), group) * share
    turned = pltpu.roll(bias[...], lax.rem(total - begin, total), 1)
    bias_out[...] = turned[0, :share]
    for copy in copies:
        copy.wait()


def local(
    n,
    nz,
    pooled,
    captions,
    norm_gain_vector,
    up_matrix,
    up_bias_vector,
    down_matrix,
    log_scale,
    logit_bias,
):
    rows, width = pooled.shape
    hidden_width = up_matrix.shape[1]
    nxy = n // (2 * nz)
    slice_width = -(-hidden_width // nxy // 128) * 128
    f32, bf16 = jnp.float32, jnp.bfloat16
    vmem = pl.BlockSpec(memory_space=pltpu.VMEM)
    away = pl.BlockSpec(memory_space=pltpu.HBM)
    dma = pltpu.SemaphoreType.DMA
    caption_grad, pooled_gradient, gain_grad, bias_whole = pl.pallas_call(
        functools.partial(kernel, n, nz),
        out_shape=(
            jax.ShapeDtypeStruct((rows, width), f32),
            jax.ShapeDtypeStruct((rows, width), f32),
            jax.ShapeDtypeStruct((1, width), f32),
            jax.ShapeDtypeStruct((1, slice_width), f32),
        ),
        in_specs=[away] * 6 + [vmem],
        out_specs=(vmem,) * 4,
        scratch_shapes=[
            pltpu.VMEM((rows, width), bf16),
            pltpu.VMEM((rows, width), bf16),
            pltpu.VMEM((1, width), f32),
            pltpu.VMEM((width, hidden_width), bf16),
            pltpu.VMEM((1, hidden_width), f32),
            pltpu.VMEM((hidden_width, width), bf16),
            pltpu.VMEM((2, 10, rows, width), bf16),
            pltpu.VMEM((rows, width), f32),
            pltpu.VMEM((rows, width), bf16),
            pltpu.VMEM((rows, hidden_width), f32),
            pltpu.VMEM((rows, width), f32),
            pltpu.VMEM((rows, width), f32),
            pltpu.VMEM((rows, width), bf16),
            pltpu.VMEM((rows, width), f32),
            pltpu.VMEM((rows, width), f32),
            pltpu.VMEM((nxy, 1, width + slice_width), f32),
            pltpu.VMEM((nxy, 1, width + slice_width), f32),
            pltpu.VMEM((2 * nz, 1, width + slice_width), f32),
            dma((CHUNKS,)),
            dma((3 + 2 * PARTS,)),
            dma((2, 8, CHUNKS)),
            dma((2, 8, CHUNKS)),
            dma((nxy - 1,)),
            dma((nxy - 1,)),
            dma((2 * nz - 1,)),
            dma((2 * nz - 1,)),
        ],
        compiler_params=pltpu.CompilerParams(
            collective_id=0, has_side_effects=True, vmem_limit_bytes=48 * 2**20
        ),
    )(
        *(
            pltpu.with_memory_space_constraint(array, pltpu.HBM)
            for array in (
                pooled,
                captions,
                norm_gain_vector,
                up_matrix,
                up_bias_vector,
                down_matrix,
            )
        ),
        jnp.where(lax.broadcasted_iota(jnp.int32, (2, 128), 0) == 0, log_scale, logit_bias),
    )
    return pl.pallas_call(
        functools.partial(finish, 2 * nz),
        out_shape=(
            jax.ShapeDtypeStruct((rows, width), f32),
            jax.ShapeDtypeStruct((rows, width), f32),
            jax.ShapeDtypeStruct((width,), f32),
            jax.ShapeDtypeStruct((hidden_width // n,), f32),
        ),
        in_specs=[vmem] * 4,
        out_specs=(away, away, away, vmem),
        scratch_shapes=[dma((2 * CHUNKS + 1,))],
        compiler_params=pltpu.CompilerParams(vmem_limit_bytes=4 * 2**20),
    )(caption_grad, pooled_gradient, gain_grad, bias_whole)


def solution(mesh, nz=8):
    placed = (P("dp", None), P("dp", None), P(), P(), P(), P(), P(), P())
    return jax.shard_map(
        functools.partial(local, mesh.shape["dp"], nz),
        mesh=mesh,
        in_specs=placed,
        out_specs=(P("dp", None), P("dp", None), P(), P("dp")),
        check_vma=False,
    )
```

```python
import functools

import jax
import jax.numpy as jnp
from jax import lax
from jax.experimental import pallas as pl
from jax.experimental.pallas import tpu as pltpu
from jax.sharding import PartitionSpec as P

MESH = pl.DeviceIdType.MESH
EPS = 1e-06
CHUNKS = 4
PARTS = 3
NT = (((1,), (1,)), ((), ()))
BEHIND, AHEAD, FAR_BEHIND, FAR_AHEAD, SIBLING, SIB_BEHIND, SIB_AHEAD, SIB_FAR = range(8)


def dot(a, b, dims=(((1,), (0,)), ((), ()))):
    return lax.dot_general(a, b, dims, preferred_element_type=jnp.float32)


def kernel(
    n,
    nz,
    pooled_hbm,
    captions_hbm,
    gain_hbm,
    up_hbm,
    bias_hbm,
    down_hbm,
    scalars,
    caption_out,
    pooled_out,
    gain_out,
    bias_out,
    pooled,
    captions,
    gain,
    up,
    bias,
    down,
    up_turned,
    down_turned,
    blocks,
    xhat,
    normed,
    slope,
    unit,
    text_unit,
    dembed,
    acc,
    dtext,
    partial,
    plane,
    line,
    caption_sem,
    load_sem,
    send_sem,
    recv_sem,
    plane_send,
    plane_recv,
    line_send,
    line_recv,
):
    rows, width = pooled.shape
    hidden_width = up.shape[1]
    nxy = n // (2 * nz)
    part = rows // CHUNKS
    group = 2 * nz
    slice_width = hidden_width // nxy
    me = lax.axis_index("dp")
    core = lax.rem(me, 2)
    xy = me // (2 * nz)
    sibling = me + 1 - 2 * core
    ahead, behind = lax.rem(me + 2, n), lax.rem(me + n - 2, n)
    plane_peers = [lax.rem(me + 2 * nz * k, n) for k in range(1, nxy)]
    place = lax.rem(me, group)
    line_peers = [xy * group + lax.rem(place + k, group) for k in range(1, group)]

    barrier = pltpu.get_barrier_semaphore()
    greeted = [ahead, behind] + plane_peers + line_peers
    for peer in greeted:
        pl.semaphore_signal(barrier, inc=1, device_id=(peer,), device_id_type=MESH)

    wide = hidden_width // PARTS
    loads = [
        pltpu.make_async_copy(pooled_hbm, pooled, load_sem.at[0]),
        pltpu.make_async_copy(gain_hbm, gain.at[0], load_sem.at[1]),
        pltpu.make_async_copy(bias_hbm, bias.at[0], load_sem.at[2]),
    ]
    up_loads, down_loads = [], []
    for p in range(PARTS):
        span = pl.ds(p * wide, wide)
        up_loads.append(
            pltpu.make_async_copy(up_hbm.at[:, span], up.at[:, span], load_sem.at[3 + 2 * p])
        )
        down_loads.append(
            pltpu.make_async_copy(down_hbm.at[span], down.at[span], load_sem.at[4 + 2 * p])
        )
        loads += [up_loads[-1], down_loads[-1]]
    caption_loads = []
    for c in range(CHUNKS):
        span = pl.ds(c * part, part)
        caption_loads.append(
            pltpu.make_async_copy(captions_hbm.at[span], captions.at[span], caption_sem.at[c])
        )
    for load in caption_loads + loads:
        load.start()

    def move(kind, side, source, target, device, c):
        span = pl.ds(c * part, part)
        return pltpu.make_async_remote_copy(
            src_ref=blocks.at[side, source, span],
            dst_ref=blocks.at[side, target, span],
            send_sem=send_sem.at[side, kind, c],
            recv_sem=recv_sem.at[side, kind, c],
            device_id=(device,),
            device_id_type=MESH,
        )

    def route(kind, side, c):
        if kind == BEHIND:
            return move(kind, side, 4 + core, 2 + core, ahead, c)
        if kind == AHEAD:
            return move(kind, side, 4 + core, 6 + core, behind, c)
        if kind == FAR_BEHIND:
            return move(kind, side, 2 + core, core, ahead, c)
        if kind == FAR_AHEAD:
            return move(kind, side, 6 + core, 8 + core, behind, c)
        if kind == SIBLING:
            return move(kind, side, 4 + core, 4 + core, sibling, c)
        if kind == SIB_BEHIND:
            return move(kind, side, 2 + core, 2 + core, sibling, c)
        if kind == SIB_AHEAD:
            return move(kind, side, 6 + core, 6 + core, sibling, c)
        return move(kind, side, 8 - 7 * core, 8 - 7 * core, sibling, c)

    def start(kinds, side, c):
        for kind in kinds:
            route(kind, side, c).start()

    def arrived(kinds, side, c):
        for kind in kinds:
            route(kind, side, c).wait_recv()

    TEXT, IMAGE = 0, 1
    first, second = range(CHUNKS // 2), range(CHUNKS // 2, CHUNKS)
    text_norms = []
    for c in range(CHUNKS):
        caption_loads[c].wait()
        span = pl.ds(c * part, part)
        text = captions[span].astype(jnp.float32)
        text_norms.append(jnp.sqrt(jnp.sum(text * text, axis=1, keepdims=True) + EPS))
        text_unit[span] = text / text_norms[c]
        blocks[TEXT, 4 + core, span] = text_unit[span].astype(jnp.bfloat16)
        if c == 0:
            pl.semaphore_wait(barrier, len(greeted))
        start([BEHIND, AHEAD] if c in first else [], TEXT, c)
    text_norm = jnp.concatenate(text_norms, axis=0)

    for load in loads[:3]:
        load.wait()
    scale = jnp.exp(jnp.broadcast_to(scalars[0:1, 0:1], (rows, 2 * rows)))
    scale_column = scale[:, :1]
    offset = scalars[1:2, 0:1]
    feats = pooled[...].astype(jnp.float32)
    centered = feats - jnp.mean(feats, axis=1, keepdims=True)
    variance = jnp.mean(centered * centered, axis=1, keepdims=True)
    rstd = lax.rsqrt(variance + EPS)
    xhat[...] = centered * rstd
    normed[...] = (xhat[...] * gain[...]).astype(jnp.bfloat16)
    acc[...] = feats
    for p in range(PARTS):
        span = pl.ds(p * wide, wide)
        up_loads[p].wait()
        x = dot(normed[...], up[:, span]) + bias[:, span]
        c0, c1 = 0.7978845608028654, 0.044715
        square = x * x
        t = jnp.tanh(c0 * x * (1.0 + c1 * square))
        slope[:, span] = 0.5 * (1.0 + t) + (0.5 * c0) * x * (1.0 - t * t) * (
            1.0 + (3.0 * c1) * square
        )
        hidden = (0.5 * x * (1.0 + t)).astype(jnp.bfloat16)
        down_loads[p].wait()
        acc[...] += dot(hidden, down[span])
        if p == 0:
            for c in second:
                start([BEHIND, AHEAD], TEXT, c)
            for c in range(CHUNKS):
                start([SIBLING], TEXT, c)
    embed = acc[...]
    image_norm = jnp.sqrt(jnp.sum(embed * embed, axis=1, keepdims=True) + EPS)
    unit[...] = embed / image_norm
    blocks[IMAGE, 4 + core] = unit[...].astype(jnp.bfloat16)

    def terms(total, side, other, own_chip=False):
        logits = scale[:, : other.shape[0]] * dot(blocks[1 - side, 4 + core], other, NT) + offset
        grad = jax.nn.sigmoid(logits)
        if own_chip:
            same = (
                lax.broadcasted_iota(jnp.int32, logits.shape, 1)
                == lax.broadcasted_iota(jnp.int32, logits.shape, 0) + core * rows
            )
            grad = jnp.where(same, -jax.nn.sigmoid(-logits), grad)
        total[...] += dot(grad.astype(jnp.bfloat16), other)

    def chip(total, side, place, own_chip=False):
        terms(total, side, blocks[side, pl.ds(2 * place, 2)].reshape(2 * rows, width), own_chip)

    def far_line(total, side):
        ends = [blocks[side, core], blocks[side, 8 + core]]
        terms(total, side, jnp.concatenate(ends, axis=0))

    def far_sibling(total, side):
        terms(total, side, blocks[side, 1 + 7 * core])

    def settle(kinds, side):
        for c in range(CHUNKS):
            arrived(kinds, side, c)

    def pass_on(side, chunks):
        for c in chunks:
            arrived([BEHIND], side, c)
            start([FAR_BEHIND, SIB_BEHIND], side, c)
        for c in chunks:
            arrived([AHEAD], side, c)
            start([FAR_AHEAD, SIB_AHEAD], side, c)

    acc[...] = jnp.zeros_like(acc)
    pass_on(TEXT, first)
    for c in range(CHUNKS):
        start([SIBLING], IMAGE, c)
    settle([SIBLING], TEXT)
    chip(acc, TEXT, 2, True)
    pass_on(TEXT, second)
    settle([SIB_BEHIND, SIB_AHEAD], TEXT)
    chip(acc, TEXT, 1)
    chip(acc, TEXT, 3)
    for q in range(0, width, rows):
        up_turned[:, q : q + rows] = up[q : q + rows].T
    for kind, far in ((BEHIND, FAR_BEHIND), (AHEAD, FAR_AHEAD)):
        for c in range(CHUNKS):
            route(far, TEXT, c).wait_send()
        for c in first:
            start([kind], IMAGE, c)
    for q in range(0, hidden_width, rows):
        down_turned[:, q : q + rows] = down[q : q + rows].T
    for c in second:
        start([BEHIND, AHEAD], IMAGE, c)
    for c in range(CHUNKS):
        arrived([FAR_BEHIND, FAR_AHEAD], TEXT, c)
        start([SIB_FAR], TEXT, c)
    far_line(acc, TEXT)
    settle([SIB_FAR], TEXT)
    far_sibling(acc, TEXT)

    dimage = scale_column * acc[...]
    along = jnp.sum(unit[...] * dimage, axis=1, keepdims=True)
    dembed[...] = ((dimage - unit[...] * along) / image_norm).astype(jnp.bfloat16)
    acc[...] = jnp.zeros_like(acc)
    pass_on(IMAGE, first)
    bias_parts = bias
    for p in range(PARTS):
        span = pl.ds(p * wide, wide)
        dpre = (dot(dembed[...], down_turned[:, span]) * slope[:, span]).astype(jnp.bfloat16)
        bias_parts[:, span] = jnp.sum(dpre.astype(jnp.float32), axis=0, keepdims=True)
        acc[...] += dot(dpre, up_turned[span])

    partial[:, :, :width] = jnp.broadcast_to(
        jnp.sum(acc[...] * xhat[...], axis=0, keepdims=True)[None], (nxy, 1, width)
    )
    for q in range(nxy):
        partial[q, :, width : width + slice_width] = bias_parts[
            :, q * slice_width : (q + 1) * slice_width
        ]

    def in_plane(k):
        return pltpu.make_async_remote_copy(
            src_ref=partial.at[lax.rem(xy + k + 1, nxy)],
            dst_ref=plane.at[xy],
            send_sem=plane_send.at[k],
            recv_sem=plane_recv.at[k],
            device_id=(plane_peers[k],),
            device_id_type=MESH,
        )

    def in_line(k):
        return pltpu.make_async_remote_copy(
            src_ref=line.at[place],
            dst_ref=line.at[place],
            send_sem=line_send.at[k],
            recv_sem=line_recv.at[k],
            device_id=(line_peers[k],),
            device_id_type=MESH,
        )

    for k in range(nxy - 1):
        in_plane(k).start()
    plane[xy] = partial[xy]
    pass_on(IMAGE, second)

    dxhat = acc[...] * gain[...]
    mean1 = jnp.mean(dxhat, axis=1, keepdims=True)
    mean2 = jnp.mean(dxhat * xhat[...], axis=1, keepdims=True)
    pooled_out[...] = dembed[...].astype(jnp.float32) + rstd * (
        dxhat - mean1 - xhat[...] * mean2
    )
    dtext[...] = jnp.zeros_like(dtext)
    settle([SIBLING], IMAGE)
    chip(dtext, IMAGE, 2, True)
    settle([SIB_BEHIND, SIB_AHEAD], IMAGE)
    chip(dtext, IMAGE, 1)
    chip(dtext, IMAGE, 3)

    for k in range(nxy - 1):
        in_plane(k).wait_recv()
    line[place] = jnp.sum(plane[...], axis=0)
    for k in range(group - 1):
        in_line(k).start()

    for c in range(CHUNKS):
        arrived([FAR_BEHIND, FAR_AHEAD], IMAGE, c)
        start([SIB_FAR], IMAGE, c)
    far_line(dtext, IMAGE)
    settle([SIB_FAR], IMAGE)
    far_sibling(dtext, IMAGE)

    dcaption = scale_column * dtext[...]
    along = jnp.sum(text_unit[...] * dcaption, axis=1, keepdims=True)
    caption_out[...] = (dcaption - text_unit[...] * along) / text_norm

    for k in range(group - 1):
        in_line(k).wait_recv()
    summed = jnp.sum(line[...], axis=0)
    gain_out[...] = summed[:, :width]
    bias_out[...] = summed[:, width:]

    for side in (TEXT, IMAGE):
        for kind in range(8):
            for c in range(CHUNKS):
                if side == IMAGE or kind not in (FAR_BEHIND, FAR_AHEAD):
                    route(kind, side, c).wait_send()
    for k in range(nxy - 1):
        in_plane(k).wait_send()
    for k in range(group - 1):
        in_line(k).wait_send()


def finish(group, caption, pooled, gain, bias, caption_out, pooled_out, gain_out, bias_out, sems):
    share = bias_out.shape[0]
    part = caption.shape[0] // CHUNKS
    copies = [pltpu.make_async_copy(gain.at[0], gain_out, sems.at[2 * CHUNKS])]
    for c in range(CHUNKS):
        span = pl.ds(c * part, part)
        copies += [
            pltpu.make_async_copy(caption.at[span], caption_out.at[span], sems.at[2 * c]),
            pltpu.make_async_copy(pooled.at[span], pooled_out.at[span], sems.at[2 * c + 1]),
        ]
    for copy in copies:
        copy.start()
    total = bias.shape[1]
    begin = lax.rem(lax.axis_index("dp"), group) * share
    turned = pltpu.roll(bias[...], lax.rem(total - begin, total), 1)
    bias_out[...] = turned[0, :share]
    for copy in copies:
        copy.wait()


def local(
    n,
    nz,
    pooled,
    captions,
    norm_gain_vector,
    up_matrix,
    up_bias_vector,
    down_matrix,
    log_scale,
    logit_bias,
):
    rows, width = pooled.shape
    hidden_width = up_matrix.shape[1]
    nxy = n // (2 * nz)
    slice_width = -(-hidden_width // nxy // 128) * 128
    f32, bf16 = jnp.float32, jnp.bfloat16
    vmem = pl.BlockSpec(memory_space=pltpu.VMEM)
    away = pl.BlockSpec(memory_space=pltpu.HBM)
    dma = pltpu.SemaphoreType.DMA
    caption_grad, pooled_gradient, gain_grad, bias_whole = pl.pallas_call(
        functools.partial(kernel, n, nz),
        out_shape=(
            jax.ShapeDtypeStruct((rows, width), f32),
            jax.ShapeDtypeStruct((rows, width), f32),
            jax.ShapeDtypeStruct((1, width), f32),
            jax.ShapeDtypeStruct((1, slice_width), f32),
        ),
        in_specs=[away] * 6 + [vmem],
        out_specs=(vmem,) * 4,
        scratch_shapes=[
            pltpu.VMEM((rows, width), bf16),
            pltpu.VMEM((rows, width), bf16),
            pltpu.VMEM((1, width), f32),
            pltpu.VMEM((width, hidden_width), bf16),
            pltpu.VMEM((1, hidden_width), f32),
            pltpu.VMEM((hidden_width, width), bf16),
            pltpu.VMEM((hidden_width, width), bf16),
            pltpu.VMEM((width, hidden_width), bf16),
            pltpu.VMEM((2, 10, rows, width), bf16),
            pltpu.VMEM((rows, width), f32),
            pltpu.VMEM((rows, width), bf16),
            pltpu.VMEM((rows, hidden_width), f32),
            pltpu.VMEM((rows, width), f32),
            pltpu.VMEM((rows, width), f32),
            pltpu.VMEM((rows, width), bf16),
            pltpu.VMEM((rows, width), f32),
            pltpu.VMEM((rows, width), f32),
            pltpu.VMEM((nxy, 1, width + slice_width), f32),
            pltpu.VMEM((nxy, 1, width + slice_width), f32),
            pltpu.VMEM((2 * nz, 1, width + slice_width), f32),
            dma((CHUNKS,)),
            dma((3 + 2 * PARTS,)),
            dma((2, 8, CHUNKS)),
            dma((2, 8, CHUNKS)),
            dma((nxy - 1,)),
            dma((nxy - 1,)),
            dma((2 * nz - 1,)),
            dma((2 * nz - 1,)),
        ],
        compiler_params=pltpu.CompilerParams(
            collective_id=0, has_side_effects=True, vmem_limit_bytes=48 * 2**20
        ),
    )(
        *(
            pltpu.with_memory_space_constraint(array, pltpu.HBM)
            for array in (
                pooled,
                captions,
                norm_gain_vector,
                up_matrix,
                up_bias_vector,
                down_matrix,
            )
        ),
        jnp.where(lax.broadcasted_iota(jnp.int32, (2, 128), 0) == 0, log_scale, logit_bias),
    )
    return pl.pallas_call(
        functools.partial(finish, 2 * nz),
        out_shape=(
            jax.ShapeDtypeStruct((rows, width), f32),
            jax.ShapeDtypeStruct((rows, width), f32),
            jax.ShapeDtypeStruct((width,), f32),
            jax.ShapeDtypeStruct((hidden_width // n,), f32),
        ),
        in_specs=[vmem] * 4,
        out_specs=(away, away, away, vmem),
        scratch_shapes=[dma((2 * CHUNKS + 1,))],
        compiler_params=pltpu.CompilerParams(vmem_limit_bytes=4 * 2**20),
    )(caption_grad, pooled_gradient, gain_grad, bias_whole)


def solution(mesh, nz=8):
    placed = (P("dp", None), P("dp", None), P(), P(), P(), P(), P(), P())
    return jax.shard_map(
        functools.partial(local, mesh.shape["dp"], nz),
        mesh=mesh,
        in_specs=placed,
        out_specs=(P("dp", None), P("dp", None), P(), P("dp")),
        check_vma=False,
    )
```

```python
import functools

import jax
import jax.numpy as jnp
from jax import lax
from jax.experimental import pallas as pl
from jax.experimental.pallas import tpu as pltpu
from jax.sharding import PartitionSpec as P

MESH = pl.DeviceIdType.MESH
EPS = 1e-06
CHUNKS = 4
PARTS = 3
NT = (((1,), (1,)), ((), ()))
BEHIND, AHEAD, FAR_BEHIND, FAR_AHEAD, SIBLING, SIB_BEHIND, SIB_AHEAD, SIB_FAR = range(8)


def dot(a, b, dims=(((1,), (0,)), ((), ()))):
    return lax.dot_general(a, b, dims, preferred_element_type=jnp.float32)


def kernel(
    n,
    nz,
    pooled_hbm,
    captions_hbm,
    gain_hbm,
    up_hbm,
    bias_hbm,
    down_hbm,
    scalars,
    caption_out,
    pooled_out,
    gain_out,
    bias_out,
    pooled,
    captions,
    gain,
    up,
    bias,
    down,
    up_turned,
    down_turned,
    blocks,
    xhat,
    normed,
    slope,
    unit,
    text_unit,
    dembed,
    acc,
    dtext,
    partial,
    plane,
    line,
    caption_sem,
    load_sem,
    send_sem,
    recv_sem,
    plane_send,
    plane_recv,
    line_send,
    line_recv,
):
    rows, width = pooled.shape
    hidden_width = up.shape[1]
    nxy = n // (2 * nz)
    part = rows // CHUNKS
    group = 2 * nz
    slice_width = hidden_width // nxy
    me = lax.axis_index("dp")
    core = lax.rem(me, 2)
    xy = me // (2 * nz)
    sibling = me + 1 - 2 * core
    ahead, behind = lax.rem(me + 2, n), lax.rem(me + n - 2, n)

    def onward(k):
        return lax.rem(me + 2 + k * (n - 4), n)

    prompt = 1 - lax.rem(me // 2, nz) // (nz // 2)
    order = (prompt, 1 - prompt)
    plane_peers = [lax.rem(me + 2 * nz * k, n) for k in range(1, nxy)]
    place = lax.rem(me, group)
    line_peers = [xy * group + lax.rem(place + k, group) for k in range(1, group)]

    barrier = pltpu.get_barrier_semaphore()
    greeted = [ahead, behind] + plane_peers + line_peers
    for peer in greeted:
        pl.semaphore_signal(barrier, inc=1, device_id=(peer,), device_id_type=MESH)

    wide = hidden_width // PARTS
    loads = [
        pltpu.make_async_copy(pooled_hbm, pooled, load_sem.at[0]),
        pltpu.make_async_copy(gain_hbm, gain.at[0], load_sem.at[1]),
        pltpu.make_async_copy(bias_hbm, bias.at[0], load_sem.at[2]),
    ]
    up_loads, down_loads = [], []
    for p in range(PARTS):
        span = pl.ds(p * wide, wide)
        up_loads.append(
            pltpu.make_async_copy(up_hbm.at[:, span], up.at[:, span], load_sem.at[3 + 2 * p])
        )
        down_loads.append(
            pltpu.make_async_copy(down_hbm.at[span], down.at[span], load_sem.at[4 + 2 * p])
        )
        loads += [up_loads[-1], down_loads[-1]]
    caption_loads = []
    for c in range(CHUNKS):
        span = pl.ds(c * part, part)
        caption_loads.append(
            pltpu.make_async_copy(captions_hbm.at[span], captions.at[span], caption_sem.at[c])
        )
    for load in caption_loads + loads:
        load.start()

    def move(kind, side, source, target, device, c):
        span = pl.ds(c * part, part)
        return pltpu.make_async_remote_copy(
            src_ref=blocks.at[side, source, span],
            dst_ref=blocks.at[side, target, span],
            send_sem=send_sem.at[side, kind, c],
            recv_sem=recv_sem.at[side, kind, c],
            device_id=(device,),
            device_id_type=MESH,
        )

    def near(k, side, c):
        return move(BEHIND + k, side, 4 + core, 2 + 4 * k + core, onward(k), c)

    def far(k, side, c):
        return move(FAR_BEHIND + k, side, 2 + 4 * k + core, 8 * k + core, onward(k), c)

    def near_to_sibling(k, side, c):
        return move(SIB_BEHIND + k, side, 2 + 4 * k + core, 2 + 4 * k + core, sibling, c)

    def route(kind, side, c):
        if kind in (BEHIND, AHEAD):
            return near(kind - BEHIND, side, c)
        if kind in (FAR_BEHIND, FAR_AHEAD):
            return far(kind - FAR_BEHIND, side, c)
        if kind in (SIB_BEHIND, SIB_AHEAD):
            return near_to_sibling(kind - SIB_BEHIND, side, c)
        if kind == SIBLING:
            return move(kind, side, 4 + core, 4 + core, sibling, c)
        return move(kind, side, 8 - 7 * core, 8 - 7 * core, sibling, c)

    def start(kinds, side, c):
        for kind in kinds:
            route(kind, side, c).start()

    def arrived(kinds, side, c):
        for kind in kinds:
            route(kind, side, c).wait_recv()

    TEXT, IMAGE = 0, 1
    first, second = range(CHUNKS // 2), range(CHUNKS // 2, CHUNKS)
    text_norms = []
    for c in range(CHUNKS):
        caption_loads[c].wait()
        span = pl.ds(c * part, part)
        text = captions[span].astype(jnp.float32)
        text_norms.append(jnp.sqrt(jnp.sum(text * text, axis=1, keepdims=True) + EPS))
        text_unit[span] = text / text_norms[c]
        blocks[TEXT, 4 + core, span] = text_unit[span].astype(jnp.bfloat16)
        if c == 0:
            pl.semaphore_wait(barrier, len(greeted))
        start([BEHIND, AHEAD] if c in first else [], TEXT, c)
    text_norm = jnp.concatenate(text_norms, axis=0)

    for load in loads[:3]:
        load.wait()
    scale = jnp.exp(jnp.broadcast_to(scalars[0:1, 0:1], (rows, 2 * rows)))
    scale_column = scale[:, :1]
    offset = scalars[1:2, 0:1]
    feats = pooled[...].astype(jnp.float32)
    centered = feats - jnp.mean(feats, axis=1, keepdims=True)
    variance = jnp.mean(centered * centered, axis=1, keepdims=True)
    rstd = lax.rsqrt(variance + EPS)
    xhat[...] = centered * rstd
    normed[...] = (xhat[...] * gain[...]).astype(jnp.bfloat16)
    acc[...] = feats
    for p in range(PARTS):
        span = pl.ds(p * wide, wide)
        up_loads[p].wait()
        x = dot(normed[...], up[:, span]) + bias[:, span]
        c0, c1 = 0.7978845608028654, 0.044715
        square = x * x
        t = jnp.tanh(c0 * x * (1.0 + c1 * square))
        slope[:, span] = 0.5 * (1.0 + t) + (0.5 * c0) * x * (1.0 - t * t) * (
            1.0 + (3.0 * c1) * square
        )
        hidden = (0.5 * x * (1.0 + t)).astype(jnp.bfloat16)
        down_loads[p].wait()
        acc[...] += dot(hidden, down[span])
        if p == 0:
            for c in second:
                start([BEHIND, AHEAD], TEXT, c)
            for c in range(CHUNKS):
                start([SIBLING], TEXT, c)
    embed = acc[...]
    image_norm = jnp.sqrt(jnp.sum(embed * embed, axis=1, keepdims=True) + EPS)
    unit[...] = embed / image_norm
    blocks[IMAGE, 4 + core] = unit[...].astype(jnp.bfloat16)

    def terms(total, side, other, own_chip=False):
        logits = scale[:, : other.shape[0]] * dot(blocks[1 - side, 4 + core], other, NT) + offset
        grad = jax.nn.sigmoid(logits)
        if own_chip:
            same = (
                lax.broadcasted_iota(jnp.int32, logits.shape, 1)
                == lax.broadcasted_iota(jnp.int32, logits.shape, 0) + core * rows
            )
            grad = jnp.where(same, -jax.nn.sigmoid(-logits), grad)
        total[...] += dot(grad.astype(jnp.bfloat16), other)

    def chip(total, side, place, own_chip=False):
        terms(total, side, blocks[side, pl.ds(2 * place, 2)].reshape(2 * rows, width), own_chip)

    def far_line(total, side):
        ends = [blocks[side, core], blocks[side, 8 + core]]
        terms(total, side, jnp.concatenate(ends, axis=0))

    def far_sibling(total, side):
        terms(total, side, blocks[side, 1 + 7 * core])

    def left(kinds, side):
        for kind in kinds:
            for c in range(CHUNKS):
                route(kind, side, c).wait_send()

    def settle(kinds, side):
        for c in range(CHUNKS):
            arrived(kinds, side, c)

    def pass_on(side, chunks, directions=order):
        for k in directions:
            for c in chunks:
                near(k, side, c).wait_recv()
                far(k, side, c).start()
                near_to_sibling(k, side, c).start()

    acc[...] = jnp.zeros_like(acc)
    pass_on(TEXT, first)
    for c in range(CHUNKS):
        start([SIBLING], IMAGE, c)
    settle([SIBLING], TEXT)
    chip(acc, TEXT, 2, True)
    pass_on(TEXT, second)
    for k in order:
        near(k, IMAGE, 0).start()
    settle([SIB_BEHIND, SIB_AHEAD], TEXT)
    chip(acc, TEXT, 1)
    chip(acc, TEXT, 3)
    for q in range(0, width, rows):
        up_turned[:, q : q + rows] = up[q : q + rows].T
    for c in range(CHUNKS):
        far(prompt, TEXT, c).wait_send()
    near(prompt, IMAGE, 1).start()
    for q in range(0, hidden_width, rows):
        down_turned[:, q : q + rows] = down[q : q + rows].T
    for c in second:
        near(prompt, IMAGE, c).start()
    for c in range(CHUNKS):
        far(1 - prompt, TEXT, c).wait_send()
    for c in range(1, CHUNKS):
        near(1 - prompt, IMAGE, c).start()
    pass_on(IMAGE, first, order[:1])
    for c in range(CHUNKS):
        arrived([FAR_BEHIND, FAR_AHEAD], TEXT, c)
        start([SIB_FAR], TEXT, c)
    far_line(acc, TEXT)
    settle([SIB_FAR], TEXT)
    far_sibling(acc, TEXT)

    dimage = scale_column * acc[...]
    along = jnp.sum(unit[...] * dimage, axis=1, keepdims=True)
    dembed[...] = ((dimage - unit[...] * along) / image_norm).astype(jnp.bfloat16)
    acc[...] = jnp.zeros_like(acc)
    bias_parts = bias
    for p in range(PARTS):
        span = pl.ds(p * wide, wide)
        dpre = (dot(dembed[...], down_turned[:, span]) * slope[:, span]).astype(jnp.bfloat16)
        bias_parts[:, span] = jnp.sum(dpre.astype(jnp.float32), axis=0, keepdims=True)
        acc[...] += dot(dpre, up_turned[span])

    partial[:, :, :width] = jnp.broadcast_to(
        jnp.sum(acc[...] * xhat[...], axis=0, keepdims=True)[None], (nxy, 1, width)
    )
    for q in range(nxy):
        partial[q, :, width : width + slice_width] = bias_parts[
            :, q * slice_width : (q + 1) * slice_width
        ]

    def in_plane(k):
        return pltpu.make_async_remote_copy(
            src_ref=partial.at[lax.rem(xy + k + 1, nxy)],
            dst_ref=plane.at[xy],
            send_sem=plane_send.at[k],
            recv_sem=plane_recv.at[k],
            device_id=(plane_peers[k],),
            device_id_type=MESH,
        )

    def in_line(k):
        return pltpu.make_async_remote_copy(
            src_ref=line.at[place],
            dst_ref=line.at[place],
            send_sem=line_send.at[k],
            recv_sem=line_recv.at[k],
            device_id=(line_peers[k],),
            device_id_type=MESH,
        )

    for k in range(nxy - 1):
        in_plane(k).start()
    plane[xy] = partial[xy]
    pass_on(IMAGE, first, order[1:])
    pass_on(IMAGE, second)

    dxhat = acc[...] * gain[...]
    mean1 = jnp.mean(dxhat, axis=1, keepdims=True)
    mean2 = jnp.mean(dxhat * xhat[...], axis=1, keepdims=True)
    pooled_out[...] = dembed[...].astype(jnp.float32) + rstd * (
        dxhat - mean1 - xhat[...] * mean2
    )
    dtext[...] = jnp.zeros_like(dtext)
    settle([SIBLING], IMAGE)
    chip(dtext, IMAGE, 2, True)
    settle([SIB_BEHIND, SIB_AHEAD], IMAGE)
    chip(dtext, IMAGE, 1)
    chip(dtext, IMAGE, 3)

    for k in range(nxy - 1):
        in_plane(k).wait_recv()
    line[place] = jnp.sum(plane[...], axis=0)
    for k in range(group - 1):
        in_line(k).start()

    left([BEHIND, AHEAD, SIBLING, SIB_BEHIND, SIB_AHEAD, SIB_FAR], TEXT)
    left([BEHIND, AHEAD, SIBLING, SIB_BEHIND, SIB_AHEAD], IMAGE)
    for k in range(nxy - 1):
        in_plane(k).wait_send()
    for c in range(CHUNKS):
        arrived([FAR_BEHIND, FAR_AHEAD], IMAGE, c)
        start([SIB_FAR], IMAGE, c)
    far_line(dtext, IMAGE)
    settle([SIB_FAR], IMAGE)
    far_sibling(dtext, IMAGE)

    dcaption = scale_column * dtext[...]
    along = jnp.sum(text_unit[...] * dcaption, axis=1, keepdims=True)
    caption_out[...] = (dcaption - text_unit[...] * along) / text_norm

    for k in range(group - 1):
        in_line(k).wait_recv()
    summed = jnp.sum(line[...], axis=0)
    gain_out[...] = summed[:, :width]
    bias_out[...] = summed[:, width:]

    for kind in (FAR_BEHIND, FAR_AHEAD, SIB_FAR):
        left([kind], IMAGE)
    for k in range(group - 1):
        in_line(k).wait_send()


def finish(group, caption, pooled, gain, bias, caption_out, pooled_out, gain_out, bias_out):
    share = bias_out.shape[0]
    caption_out[...] = caption[...]
    pooled_out[...] = pooled[...]
    gain_out[...] = gain[0, :]
    total = bias.shape[1]
    begin = lax.rem(lax.axis_index("dp"), group) * share
    turned = pltpu.roll(bias[...], lax.rem(total - begin, total), 1)
    bias_out[...] = turned[0, :share]


def local(
    n,
    nz,
    pooled,
    captions,
    norm_gain_vector,
    up_matrix,
    up_bias_vector,
    down_matrix,
    log_scale,
    logit_bias,
):
    rows, width = pooled.shape
    hidden_width = up_matrix.shape[1]
    nxy = n // (2 * nz)
    slice_width = -(-hidden_width // nxy // 128) * 128
    f32, bf16 = jnp.float32, jnp.bfloat16
    vmem = pl.BlockSpec(memory_space=pltpu.VMEM)
    away = pl.BlockSpec(memory_space=pltpu.HBM)
    dma = pltpu.SemaphoreType.DMA
    caption_grad, pooled_gradient, gain_grad, bias_whole = pl.pallas_call(
        functools.partial(kernel, n, nz),
        out_shape=(
            jax.ShapeDtypeStruct((rows, width), f32),
            jax.ShapeDtypeStruct((rows, width), f32),
            jax.ShapeDtypeStruct((1, width), f32),
            jax.ShapeDtypeStruct((1, slice_width), f32),
        ),
        in_specs=[away] * 6 + [vmem],
        out_specs=(vmem,) * 4,
        scratch_shapes=[
            pltpu.VMEM((rows, width), bf16),
            pltpu.VMEM((rows, width), bf16),
            pltpu.VMEM((1, width), f32),
            pltpu.VMEM((width, hidden_width), bf16),
            pltpu.VMEM((1, hidden_width), f32),
            pltpu.VMEM((hidden_width, width), bf16),
            pltpu.VMEM((hidden_width, width), bf16),
            pltpu.VMEM((width, hidden_width), bf16),
            pltpu.VMEM((2, 10, rows, width), bf16),
            pltpu.VMEM((rows, width), f32),
            pltpu.VMEM((rows, width), bf16),
            pltpu.VMEM((rows, hidden_width), f32),
            pltpu.VMEM((rows, width), f32),
            pltpu.VMEM((rows, width), f32),
            pltpu.VMEM((rows, width), bf16),
            pltpu.VMEM((rows, width), f32),
            pltpu.VMEM((rows, width), f32),
            pltpu.VMEM((nxy, 1, width + slice_width), f32),
            pltpu.VMEM((nxy, 1, width + slice_width), f32),
            pltpu.VMEM((2 * nz, 1, width + slice_width), f32),
            dma((CHUNKS,)),
            dma((3 + 2 * PARTS,)),
            dma((2, 8, CHUNKS)),
            dma((2, 8, CHUNKS)),
            dma((nxy - 1,)),
            dma((nxy - 1,)),
            dma((2 * nz - 1,)),
            dma((2 * nz - 1,)),
        ],
        compiler_params=pltpu.CompilerParams(
            collective_id=0, has_side_effects=True, vmem_limit_bytes=48 * 2**20
        ),
    )(
        *(
            pltpu.with_memory_space_constraint(array, pltpu.HBM)
            for array in (
                pooled,
                captions,
                norm_gain_vector,
                up_matrix,
                up_bias_vector,
                down_matrix,
            )
        ),
        jnp.where(lax.broadcasted_iota(jnp.int32, (2, 128), 0) == 0, log_scale, logit_bias),
    )
    return pl.pallas_call(
        functools.partial(finish, 2 * nz),
        out_shape=(
            jax.ShapeDtypeStruct((rows, width), f32),
            jax.ShapeDtypeStruct((rows, width), f32),
            jax.ShapeDtypeStruct((width,), f32),
            jax.ShapeDtypeStruct((hidden_width // n,), f32),
        ),
        in_specs=[vmem] * 4,
        out_specs=(vmem,) * 4,
        compiler_params=pltpu.CompilerParams(vmem_limit_bytes=8 * 2**20),
    )(caption_grad, pooled_gradient, gain_grad, bias_whole)


def solution(mesh, nz=8):
    placed = (P("dp", None), P("dp", None), P(), P(), P(), P(), P(), P())
    return jax.shard_map(
        functools.partial(local, mesh.shape["dp"], nz),
        mesh=mesh,
        in_specs=placed,
        out_specs=(P("dp", None), P("dp", None), P(), P("dp")),
        check_vma=False,
    )
```
